512 devices in a mesh: blk: 32 (over y, z_hi, core), grp: 16 (over x, z_lo).
Axes of the slice: x: 4, y: 8, z: 8 (z_hi: 2, z_lo: 4; z = z_hi * 4 + z_lo), core: 2. Of those that a mesh axis runs over, the one named last changes fastest.
Arguments:
- images: bfloat16 [262144, 1152], P(('blk', 'grp')), may hold values from -0.17675781 to 0.17675781
- texts: bfloat16 [512, 1152], P(('blk', 'grp')), may hold values from -0.17675781 to 0.17675781
- labels: int32 [262144], P(('blk', 'grp')), may hold values from 0 to 511
- log_scale: float32 [1], replicated, may hold values from 3.9 to 4.6
- bias: float32 [1], replicated, may hold values from -6 to -2
- loss_scale: float32 [1], replicated, may hold values from 8192 to 32768
Outputs:
- grad_image: bfloat16 [262144, 1152], P(('blk', 'grp'))
- grad_text: bfloat16 [512, 1152], P(('blk', 'grp'))
The draws below stay inside these ranges and needn't reach their ends.
Inputs may be any that keep to these rules, and one draw needn't show every extreme that they name: labels[i] is the caption paired with frame i; a caption has many frames.
All inputs are finite; a program needn't handle non-finite values.
Results may differ from the reference program's by a relative error of at most 0.0047.
Values may be sent and summed in bfloat16 or wider, within the bound.
No kernel may reach another device: no remote copies, remote signals or barrier semaphores. Data moves between devices by JAX's collectives and lax.ppermute only.
A program may use at most 64 MiB of HBM per device.

```python
import math
import jax
import jax.numpy as jnp
from jax import lax

D = 1152
IMAGES = 262144
TEXTS = 512


def touch_ends(entries, own_key, smallest, top_value):
    longest = entries.shape.index(max(entries.shape))
    spots = []
    for shift in (0, 1):
        where = [jax.random.randint(jax.random.fold_in(own_key, axis), (), 0, length) for axis, length in enumerate(entries.shape)]
        where[longest] = (where[longest] + shift) % entries.shape[longest]
        spots.append(tuple(where))
    return entries.at[spots[0]].set(smallest).at[spots[1]].set(top_value)


def levels(stream_key, shape, pieces, smallest, largest):
    def one(axis_at, shards_of):
        steps = jax.random.uniform(jax.random.fold_in(jax.random.fold_in(stream_key, 6), axis_at), (shards_of,), jnp.float32, smallest / len(pieces), largest / len(pieces))
        return jnp.repeat(jnp.exp(steps), shape[axis_at] // shards_of).reshape((-1,) + (1,) * (len(shape) - axis_at - 1))

    loudness = one(*pieces[0])
    for cut in pieces[1:]:
        loudness = loudness * one(*cut)
    return loudness


def noise(stream_key, dims, scale, limit, pieces=(), kind=jnp.bfloat16):
    factor_of = levels(stream_key, dims, pieces, -0.22, 0.18) if pieces else 1.0
    entries = jax.random.normal(stream_key, dims, jnp.float32) * scale * factor_of
    return jnp.minimum(jnp.maximum(entries, -limit), limit).astype(kind)


def setup_inputs(seed: int = 0) -> dict:
    seeds = jax.random.split(jax.random.key(seed), 7)
    images = noise(seeds[0], (IMAGES, D), (D ** -0.5), 0.17675781, ((0, 512),))
    texts = noise(seeds[1], (TEXTS, D), (D ** -0.5), 0.17675781, ((0, 512),))
    labels = touch_ends(jax.random.randint(seeds[2], (IMAGES,), 0, TEXTS), jax.random.fold_in(seeds[2], 1), 0, TEXTS - 1).astype(jnp.int32)
    log_scale = jnp.clip(jax.random.uniform(seeds[3], (1,), jnp.float32, 3.9, 4.6), 3.9, 4.6)
    bias = jnp.clip(jax.random.uniform(seeds[4], (1,), jnp.float32, -6.0, -2.0), -6.0, -2.0)
    loss_scale = jnp.clip(jnp.exp(jax.random.uniform(seeds[5], (1,), jnp.float32, math.log(8192.0), math.log(32768.0))), 8192.0, 32768.0)
    return {"images": images, "texts": texts, "labels": labels, "log_scale": log_scale, "bias": bias, "loss_scale": loss_scale}


def reference(images, texts, labels, log_scale, bias, loss_scale):
    factor = jnp.exp(log_scale[0])
    weight = factor * loss_scale[0] / IMAGES
    block_rows = math.gcd(IMAGES, 4096)
    image_blocks = images.reshape(IMAGES // block_rows, block_rows, D)
    label_blocks = labels.reshape(IMAGES // block_rows, block_rows)
    columns = jnp.arange(TEXTS, dtype=jnp.int32)

    def one_block(text_grad, pair):
        image_rows, label_rows = pair
        logits = factor * lax.dot_general(image_rows, texts, (((1,), (1,)), ((), ())), preferred_element_type=jnp.float32) + bias[0]
        pair_sign = jnp.where(label_rows[:, None] == columns[None, :], 1.0, -1.0).astype(jnp.float32)
        coefficient = (-pair_sign * jax.nn.sigmoid(-pair_sign * logits) * weight).astype(jnp.bfloat16)
        grad_rows = jnp.dot(coefficient, texts, preferred_element_type=jnp.float32).astype(jnp.bfloat16)
        text_grad = text_grad + lax.dot_general(coefficient, image_rows, (((0,), (0,)), ((), ())), preferred_element_type=jnp.float32)
        return text_grad, grad_rows

    text_grad, grad_blocks = lax.scan(one_block, jnp.zeros((TEXTS, D), jnp.float32), (image_blocks, label_blocks))
    return grad_blocks.reshape(IMAGES, D), text_grad.astype(jnp.bfloat16)
```

```python
import jax
import jax.numpy as jnp
from jax import lax
from jax.sharding import Mesh
from jax.sharding import PartitionSpec as P

WIDE = ("far", "near")


def swap_cores(array):
    return lax.ppermute(array, "core", [(0, 1), (1, 0)])


def exchange(array):
    return lax.all_to_all(array, WIDE, 0, 0, tiled=True)


def coefficients(images, labels, block, columns, factor, offset, weight):
    logits = (
        factor
        * lax.dot_general(
            images, block, (((1,), (1,)), ((), ())), preferred_element_type=jnp.float32
        )
        + offset
    )
    pair_sign = jnp.where(labels[:, None] == columns[None, :], 1.0, -1.0).astype(jnp.float32)
    return (-pair_sign * jax.nn.sigmoid(-pair_sign * logits) * weight).astype(jnp.bfloat16)


def text_part(coefficient, images):
    return lax.dot_general(
        coefficient, images, (((0,), (0,)), ((), ())), preferred_element_type=jnp.float32
    )


def local(images, texts, labels, log_scale, bias, loss_scale):
    far, cores, near = (lax.axis_size(name) for name in ("far", "core", "near"))
    core = lax.axis_index("core")
    factor = jnp.exp(log_scale[0])
    offset = bias[0]
    weight = factor * loss_scale[0] / (images.shape[0] * far * cores * near)
    shared = far * near

    place = jnp.arange(shared, dtype=jnp.int32)
    first = place // near * (cores * near) + place % near
    columns_mine = first + core * near
    columns_other = first + (1 - core) * near

    with jax.named_scope("gather_texts"):
        mine = exchange(jnp.broadcast_to(texts, (shared, texts.shape[1])))
        other = swap_cores(mine)

    with jax.named_scope("coefficients"):
        coef_mine = coefficients(images, labels, mine, columns_mine, factor, offset, weight)
        coef_other = coefficients(images, labels, other, columns_other, factor, offset, weight)

    with jax.named_scope("text_grad"):
        given = swap_cores(text_part(coef_other, images).astype(jnp.bfloat16))
        kept = text_part(coef_mine, images)
        pair = (kept + given.astype(jnp.float32)).astype(jnp.bfloat16)
        parts = exchange(pair)
        text_grad = jnp.sum(parts.astype(jnp.float32), axis=0, keepdims=True)

    with jax.named_scope("image_grad"):
        image_grad = jnp.dot(
            jnp.concatenate([coef_mine, coef_other], 1),
            jnp.concatenate([mine, other], 0),
            preferred_element_type=jnp.float32,
        )
    return (image_grad.astype(jnp.bfloat16), text_grad.astype(jnp.bfloat16))


def solution(mesh):
    blk, grp = mesh.devices.shape
    fine = Mesh(mesh.devices.reshape(blk // 2, 2, grp), ("far", "core", "near"))
    rows = ("far", "core", "near")
    placed = (P(rows, None), P(rows, None), P(rows), P(), P(), P())
    return jax.shard_map(
        local,
        mesh=fine,
        in_specs=placed,
        out_specs=(P(rows, None), P(rows, None)),
        check_vma=False,
    )
```

```python
import jax
import jax.numpy as jnp
from jax import lax
from jax.experimental import pallas as pl
from jax.experimental.pallas import tpu as pltpu
from jax.sharding import Mesh
from jax.sharding import PartitionSpec as P

WIDE = ("far", "zl", "x")
IN_PIECES = 2
OUT_PIECES = 4
HBM = pl.BlockSpec(memory_space=pltpu.HBM)
VMEM = pl.BlockSpec(memory_space=pltpu.VMEM)
SMEM = pl.BlockSpec(memory_space=pltpu.SMEM)
PARAMS = pltpu.CompilerParams(vmem_limit_bytes=24 << 20)


def swap_cores(*arrays):
    return [lax.ppermute(array, "core", [(0, 1), (1, 0)]) for array in arrays]


def exchange(array):
    return lax.all_to_all(array, WIDE, 0, 0, tiled=True)


def dot(left, right, along):
    return lax.dot_general(
        left, right, ((along[:1], along[1:]), ((), ())), preferred_element_type=jnp.float32
    )


def put(space, *arrays):
    return [pltpu.with_memory_space_constraint(array, space) for array in arrays]


def cost(flops, moved, exps=0):
    return pl.CostEstimate(flops=flops, bytes_accessed=moved, transcendentals=exps)


def repeat_kernel(row, out):
    width = out.shape[2]
    values = row[...].astype(jnp.float32)
    halves = jnp.concatenate([values[:, :width], values[:, width:]], 0).astype(out.dtype)
    out[...] = jnp.broadcast_to(halves[None], out.shape)


def split_kernel(whole, *refs):
    *pieces, held, sems, out_sems = refs
    size = pieces[0].shape[0]
    loads, stores = [], []
    for index, piece in enumerate(pieces):
        span = pl.ds(index * size, size)
        loads.append(pltpu.make_async_copy(whole.at[span], held.at[index], sems.at[index]))
        stores.append(pltpu.make_async_copy(held.at[index], piece, out_sems.at[index]))
    for load in loads:
        load.start()
    for load, store in zip(loads, stores):
        load.wait()
        store.start()
    for store in stores:
        store.wait()


def coefficient_kernel(scalars, columns, halves, labels, other_labels, images, *refs):
    *others, block_out, coef_out, other_coef_out, part = refs[:-6]
    own, block, coef, other_coef, sem, out_sems = refs[-6:]
    load = pltpu.make_async_copy(images, own, sem)
    load.start()
    factor, offset, weight = scalars[0], scalars[1], scalars[2]
    block[...] = halves[...].reshape(block.shape)
    stores = [pltpu.make_async_copy(block, block_out, out_sems.at[0])]
    stores[0].start()
    load.wait()

    def piece(frames, paired):
        logits = factor * dot(block[...], frames, (1, 1)) + offset
        pair_sign = jnp.where(paired == columns[...], 1.0, -1.0).astype(jnp.float32)
        value = -pair_sign * jax.nn.sigmoid(-pair_sign * logits) * weight
        value = value.astype(jnp.bfloat16)
        return value, dot(value, frames, (1, 0))

    coef[...], total = piece(own[...], labels[...])
    stores.append(pltpu.make_async_copy(coef, coef_out, out_sems.at[1]))
    stores[1].start()
    for index, frames in enumerate(others):
        size = frames.shape[0]
        span = pl.ds(index * size, size)
        other_coef[:, span], term = piece(frames[...], other_labels[:, span])
        total = total + term
    stores.append(pltpu.make_async_copy(other_coef, other_coef_out, out_sems.at[2]))
    stores[2].start()
    width = part.shape[2]
    part[:, 0, :] = total[:, :width].astype(part.dtype)
    part[:, 1, :] = total[:, width:].astype(part.dtype)
    for store in stores:
        store.wait()


def partial_kernel(coef_in, block_in, *refs):
    *outs, coef, block, held, in_sems, sems = refs
    size = outs[0].shape[0]
    loads = [
        pltpu.make_async_copy(coef_in, coef, in_sems.at[0]),
        pltpu.make_async_copy(block_in, block, in_sems.at[1]),
    ]
    for load in loads:
        load.start()
    for load in loads:
        load.wait()
    stores = []
    for index, out in enumerate(outs):
        held[index] = dot(coef[:, pl.ds(index * size, size)], block[...], (0, 0))
        stores.append(pltpu.make_async_copy(held.at[index], out, sems.at[index]))
        stores[-1].start()
    for store in stores:
        store.wait()


def image_kernel(coef_in, block_in, *refs):
    *given, out, coef, block, held, result, in_sems, sems, out_sems = refs
    size = given[0].shape[0]
    loads = [
        pltpu.make_async_copy(coef_in, coef, in_sems.at[0]),
        pltpu.make_async_copy(block_in, block, in_sems.at[1]),
    ]
    copies = [
        pltpu.make_async_copy(source, held.at[index], sems.at[index])
        for index, source in enumerate(given)
    ]
    for load in loads + copies:
        load.start()
    for load in loads:
        load.wait()
    stores = []
    for index, copy in enumerate(copies):
        span = pl.ds(index * size, size)
        share = dot(coef[:, span], block[...], (0, 0))
        copy.wait()
        result[index] = (share + held[index]).astype(result.dtype)
        stores.append(pltpu.make_async_copy(result.at[index], out.at[span], out_sems.at[index]))
        stores[-1].start()
    for store in stores:
        store.wait()


def local(images, texts, labels, log_scale, bias, loss_scale):
    far, cores, x, zl = (lax.axis_size(name) for name in ("far", "core", "x", "zl"))
    core = lax.axis_index("core")
    rows = images.shape[0]
    width = texts.shape[1]
    shared = far * x * zl
    factor = jnp.exp(log_scale[0])
    weight = factor * loss_scale[0] / (rows * shared * cores)
    scalars = jnp.stack([factor, bias[0], weight])
    flops = 2 * shared * rows * width

    place = jnp.arange(shared, dtype=jnp.int32)
    columns = place // (x * zl) * (cores * x * zl) + core * x * zl
    columns = columns + place % x * zl + place // x % zl

    with jax.named_scope("gather_texts"):
        halves = pl.pallas_call(
            repeat_kernel,
            out_shape=pltpu.VMEM((shared, 2, width // 2), texts.dtype),
            in_specs=[VMEM],
            out_specs=VMEM,
            compiler_params=PARAMS,
        )(texts)
        halves = exchange(halves)

    with jax.named_scope("swap_images"):
        pieces = pl.pallas_call(
            split_kernel,
            out_shape=[pltpu.HBM((rows // IN_PIECES, width), images.dtype)] * IN_PIECES,
            in_specs=[HBM],
            out_specs=[HBM] * IN_PIECES,
            scratch_shapes=[
                pltpu.VMEM((IN_PIECES, rows // IN_PIECES, width), images.dtype),
                pltpu.SemaphoreType.DMA((IN_PIECES,)),
                pltpu.SemaphoreType.DMA((IN_PIECES,)),
            ],
            compiler_params=PARAMS,
            cost_estimate=cost(0, 4 * rows * width),
        )(*put(pltpu.HBM, images))
        *others, labels_other = swap_cores(*pieces, labels)

    with jax.named_scope("coefficients"):
        block, coef, coef_other, part = pl.pallas_call(
            coefficient_kernel,
            out_shape=(
                pltpu.HBM((shared, width), jnp.bfloat16),
                pltpu.HBM((shared, rows), jnp.bfloat16),
                pltpu.HBM((shared, rows), jnp.bfloat16),
                pltpu.VMEM((shared, 2, width // 2), jnp.bfloat16),
            ),
            in_specs=[SMEM] + [VMEM] * 4 + [HBM] + [VMEM] * IN_PIECES,
            out_specs=(HBM, HBM, HBM, VMEM),
            scratch_shapes=[
                pltpu.VMEM((rows, width), jnp.bfloat16),
                pltpu.VMEM((shared, width), jnp.bfloat16),
                pltpu.VMEM((shared, rows), jnp.bfloat16),
                pltpu.VMEM((shared, rows), jnp.bfloat16),
                pltpu.SemaphoreType.DMA,
                pltpu.SemaphoreType.DMA((3,)),
            ],
            compiler_params=PARAMS,
            cost_estimate=cost(4 * flops, 4 * rows * width, 2 * shared * rows),
        )(
            scalars,
            columns[:, None],
            *put(pltpu.VMEM, halves),
            labels[None, :],
            labels_other[None, :],
            *put(pltpu.HBM, images),
            *put(pltpu.VMEM, *others),
        )

    with jax.named_scope("text_grad"):
        parts = exchange(part)
        text_grad = jnp.sum(parts.astype(jnp.float32), axis=0).reshape(1, width)

    with jax.named_scope("image_grad"):
        size = rows // OUT_PIECES
        given = pl.pallas_call(
            partial_kernel,
            out_shape=[pltpu.HBM((size, width), jnp.float32)] * OUT_PIECES,
            in_specs=[HBM, HBM],
            out_specs=[HBM] * OUT_PIECES,
            scratch_shapes=[
                pltpu.VMEM((shared, rows), jnp.bfloat16),
                pltpu.VMEM((shared, width), jnp.bfloat16),
                pltpu.VMEM((OUT_PIECES, size, width), jnp.float32),
                pltpu.SemaphoreType.DMA((2,)),
                pltpu.SemaphoreType.DMA((OUT_PIECES,)),
            ],
            compiler_params=PARAMS,
            cost_estimate=cost(flops, 4 * rows * width),
        )(*put(pltpu.HBM, coef_other, block))
        image_grad = pl.pallas_call(
            image_kernel,
            out_shape=jax.ShapeDtypeStruct((rows, width), jnp.bfloat16),
            in_specs=[HBM] * (2 + OUT_PIECES),
            out_specs=HBM,
            scratch_shapes=[
                pltpu.VMEM((shared, rows), jnp.bfloat16),
                pltpu.VMEM((shared, width), jnp.bfloat16),
                pltpu.VMEM((OUT_PIECES, size, width), jnp.float32),
                pltpu.VMEM((OUT_PIECES, size, width), jnp.bfloat16),
                pltpu.SemaphoreType.DMA((2,)),
                pltpu.SemaphoreType.DMA((OUT_PIECES,)),
                pltpu.SemaphoreType.DMA((OUT_PIECES,)),
            ],
            compiler_params=PARAMS,
            cost_estimate=cost(flops, 6 * rows * width),
        )(*put(pltpu.HBM, coef, block), *swap_cores(*given))
    return (image_grad, text_grad.astype(jnp.bfloat16))


def solution(mesh):
    blk, grp = mesh.devices.shape
    rows = ("far", "core", "x", "zl")
    fine = Mesh(mesh.devices.reshape(blk // 2, 2, 4, grp // 4), rows)
    placed = (P(rows, None), P(rows, None), P(rows), P(), P(), P())
    return jax.shard_map(
        local,
        mesh=fine,
        in_specs=placed,
        out_specs=(P(rows, None), P(rows, None)),
        check_vma=False,
    )
```

```python
import jax
import jax.numpy as jnp
from jax import lax
from jax.experimental import pallas as pl
from jax.experimental.pallas import tpu as pltpu
from jax.sharding import Mesh
from jax.sharding import PartitionSpec as P

WIDE = ("far", "zl")
IN_PIECES = 2
OUT_PIECES = 4
HBM = pl.BlockSpec(memory_space=pltpu.HBM)
VMEM = pl.BlockSpec(memory_space=pltpu.VMEM)
SMEM = pl.BlockSpec(memory_space=pltpu.SMEM)
PARAMS = pltpu.CompilerParams(vmem_limit_bytes=24 << 20)


def swap_cores(*arrays):
    return [lax.ppermute(array, "core", [(0, 1), (1, 0)]) for array in arrays]


def exchange(array, axes):
    return lax.all_to_all(array, axes, 0, 0, tiled=True)


def dot(left, right, along):
    return lax.dot_general(
        left, right, ((along[:1], along[1:]), ((), ())), preferred_element_type=jnp.float32
    )


def put(space, *arrays):
    return [pltpu.with_memory_space_constraint(array, space) for array in arrays]


def cost(flops, moved, exps=0):
    return pl.CostEstimate(flops=flops, bytes_accessed=moved, transcendentals=exps)


def repeat_kernel(row, out):
    width = out.shape[2]
    values = row[...].astype(jnp.float32)
    halves = jnp.concatenate([values[:, :width], values[:, width:]], 0).astype(out.dtype)
    out[...] = jnp.broadcast_to(halves[None], out.shape)


def spread_kernel(halves, out):
    rows = halves[...].reshape(out.shape[1:])
    for index in range(out.shape[0]):
        out[index] = rows


def gather_kernel(blocks, out):
    total = blocks[0].astype(jnp.float32)
    for index in range(1, blocks.shape[0]):
        total = total + blocks[index].astype(jnp.float32)
    width = out.shape[2]
    out[:, 0, :] = total[:, :width].astype(out.dtype)
    out[:, 1, :] = total[:, width:].astype(out.dtype)


def sum_kernel(parts, out):
    total = jnp.sum(parts[...].astype(jnp.float32), axis=0)
    width = parts.shape[2]
    out[:, :width] = total[0:1].astype(out.dtype)
    out[:, width:] = total[1:2].astype(out.dtype)


def split_kernel(whole, *refs):
    *pieces, held, sems, out_sems = refs
    size = pieces[0].shape[0]
    loads, stores = [], []
    for index, piece in enumerate(pieces):
        span = pl.ds(index * size, size)
        loads.append(pltpu.make_async_copy(whole.at[span], held.at[index], sems.at[index]))
        stores.append(pltpu.make_async_copy(held.at[index], piece, out_sems.at[index]))
    for load in loads:
        load.start()
    for load, store in zip(loads, stores):
        load.wait()
        store.start()
    for store in stores:
        store.wait()


def coefficients(block, frames, paired, columns, scalars):
    factor, offset, weight = scalars[0], scalars[1], scalars[2]
    logits = factor * dot(block, frames, (1, 1)) + offset
    own = paired == columns
    value = jax.nn.sigmoid(jnp.where(own, -logits, logits)) * jnp.where(own, -weight, weight)
    return value.astype(jnp.bfloat16)


def text_kernel(scalars, columns, texts, labels, other_labels, images, *refs):
    *others, coef, part = refs
    block = texts[...].reshape(part.shape)
    value = coefficients(block, images[...], labels[...], columns[...], scalars)
    coef[...] = value
    terms = [(value, images)]
    for index, frames in enumerate(others):
        size = frames.shape[0]
        paired = other_labels[:, pl.ds(index * size, size)]
        terms.append((coefficients(block, frames[...], paired, columns[...], scalars), frames))
    total = sum(dot(value, frames[...], (1, 0)) for value, frames in terms)
    part[...] = total.astype(part.dtype)


def image_kernel(scalars, columns, labels, coef, texts, other_texts, images, out, *scratch):
    result, out_sems = scratch
    block = texts[...].reshape(-1, texts.shape[2])
    other = other_texts[...].reshape(-1, texts.shape[2])
    value = coefficients(other, images[...], labels[...], columns[...], scalars)
    size = result.shape[1]
    stores = []
    for index in range(result.shape[0]):
        span = slice(index * size, (index + 1) * size)
        total = dot(coef[:, span], block, (0, 0)) + dot(value[:, span], other, (0, 0))
        result[index] = total.astype(result.dtype)
        target = out.at[pl.ds(index * size, size)]
        stores.append(pltpu.make_async_copy(result.at[index], target, out_sems.at[index]))
        stores[-1].start()
    for store in stores:
        store.wait()


def local(images, texts, labels, log_scale, bias, loss_scale):
    far, cores, x, zl = (lax.axis_size(name) for name in ("far", "core", "x", "zl"))
    core = lax.axis_index("core")
    rows = images.shape[0]
    width = texts.shape[1]
    shared = far * x * zl
    factor = jnp.exp(log_scale[0])
    weight = factor * loss_scale[0] / (rows * shared * cores)
    scalars = jnp.stack([factor, bias[0], weight])
    flops = 2 * shared * rows * width

    place = jnp.arange(shared, dtype=jnp.int32)
    first = place // zl % far * (cores * x * zl) + place // (far * zl) * zl + place % zl
    columns = (first + core * x * zl)[:, None]
    columns_other = (first + (1 - core) * x * zl)[:, None]
    half = width // 2
    plane = far * zl

    with jax.named_scope("gather_texts"):
        halves = pl.pallas_call(
            repeat_kernel,
            out_shape=jax.ShapeDtypeStruct((plane, 2, half), texts.dtype),
            in_specs=[VMEM],
            out_specs=VMEM,
            compiler_params=PARAMS,
        )(texts)
        halves = exchange(halves, WIDE)
        blocks = pl.pallas_call(
            spread_kernel,
            out_shape=jax.ShapeDtypeStruct((x, plane, width), texts.dtype),
            in_specs=[VMEM],
            out_specs=VMEM,
            compiler_params=PARAMS,
        )(halves)
        blocks = exchange(blocks, "x")

    with jax.named_scope("swap_images"):
        pieces = pl.pallas_call(
            split_kernel,
            out_shape=[pltpu.HBM((rows // IN_PIECES, width), images.dtype)] * IN_PIECES,
            in_specs=[HBM],
            out_specs=[HBM] * IN_PIECES,
            scratch_shapes=[
                pltpu.VMEM((IN_PIECES, rows // IN_PIECES, width), images.dtype),
                pltpu.SemaphoreType.DMA((IN_PIECES,)),
                pltpu.SemaphoreType.DMA((IN_PIECES,)),
            ],
            compiler_params=PARAMS,
            cost_estimate=cost(0, 4 * rows * width),
        )(*put(pltpu.HBM, images))
        *others, labels_other = swap_cores(*pieces, labels)

    with jax.named_scope("coefficients"):
        coef, part = pl.pallas_call(
            text_kernel,
            out_shape=(
                jax.ShapeDtypeStruct((shared, rows), jnp.bfloat16),
                jax.ShapeDtypeStruct((shared, width), jnp.bfloat16),
            ),
            in_specs=[SMEM] + [VMEM] * (5 + IN_PIECES),
            out_specs=(VMEM, VMEM),
            compiler_params=PARAMS,
            cost_estimate=cost(4 * flops, 4 * rows * width, 2 * shared * rows),
        )(
            scalars,
            columns,
            *put(pltpu.VMEM, blocks),
            labels[None, :],
            labels_other[None, :],
            *put(pltpu.VMEM, images, *others),
        )

    with jax.named_scope("text_grad"):
        blocks_grad = exchange(part.reshape(x, plane, width), "x")
        summed = pl.pallas_call(
            gather_kernel,
            out_shape=jax.ShapeDtypeStruct((plane, 2, half), jnp.bfloat16),
            in_specs=[VMEM],
            out_specs=VMEM,
            compiler_params=PARAMS,
        )(blocks_grad)
        text_grad = pl.pallas_call(
            sum_kernel,
            out_shape=jax.ShapeDtypeStruct((1, width), jnp.bfloat16),
            in_specs=[VMEM],
            out_specs=VMEM,
            compiler_params=PARAMS,
        )(exchange(summed, WIDE))

    with jax.named_scope("image_grad"):
        (blocks_other,) = swap_cores(blocks)
        image_grad = pl.pallas_call(
            image_kernel,
            out_shape=jax.ShapeDtypeStruct((rows, width), jnp.bfloat16),
            in_specs=[SMEM] + [VMEM] * 6,
            out_specs=HBM,
            scratch_shapes=[
                pltpu.VMEM((OUT_PIECES, rows // OUT_PIECES, width), jnp.bfloat16),
                pltpu.SemaphoreType.DMA((OUT_PIECES,)),
            ],
            compiler_params=PARAMS,
            cost_estimate=cost(3 * flops, 6 * rows * width, shared * rows),
        )(
            scalars,
            columns_other,
            labels[None, :],
            coef,
            blocks,
            blocks_other,
            images,
        )
    return (image_grad, text_grad)


def solution(mesh):
    blk, grp = mesh.devices.shape
    rows = ("far", "core", "x", "zl")
    fine = Mesh(mesh.devices.reshape(blk // 2, 2, 4, grp // 4), rows)
    placed = (P(rows, None), P(rows, None), P(rows), P(), P(), P())
    return jax.shard_map(
        local,
        mesh=fine,
        in_specs=placed,
        out_specs=(P(rows, None), P(rows, None)),
        check_vma=False,
    )
```

```python
import functools

import jax
import jax.numpy as jnp
from jax import lax
from jax.experimental import pallas as pl
from jax.experimental.pallas import tpu as pltpu
from jax.sharding import Mesh
from jax.sharding import PartitionSpec as P

WIDE = ("far", "zl")
IN_PIECES = 2
OUT_PIECES = 2
TEXT_PIECES = 2
TAIL = 16
HOLD = 1 << 34
HBM = pl.BlockSpec(memory_space=pltpu.HBM)
ANY = pl.BlockSpec(memory_space=pl.ANY)
SMEM = pl.BlockSpec(memory_space=pltpu.SMEM)
VMEM = pl.BlockSpec(memory_space=pltpu.VMEM)
PARAMS = pltpu.CompilerParams(vmem_limit_bytes=24 << 20)


def swap_cores(*arrays):
    return [lax.ppermute(array, "core", [(0, 1), (1, 0)]) for array in arrays]


def exchange(array, axes):
    return lax.all_to_all(array, axes, 0, 0, tiled=True)


def dot(left, right, along):
    return lax.dot_general(
        left, right, ((along[:1], along[1:]), ((), ())), preferred_element_type=jnp.float32
    )


def put(space, *arrays):
    return [pltpu.with_memory_space_constraint(array, space) for array in arrays]


def cost(flops, moved, exps=0):
    return pl.CostEstimate(flops=flops, bytes_accessed=moved, transcendentals=exps)


def repeat_kernel(row, out):
    width = out.shape[2]
    values = row[...].astype(jnp.float32)
    halves = jnp.concatenate([values[:, :width], values[:, width:]], 0).astype(out.dtype)
    out[...] = jnp.broadcast_to(halves[None], out.shape)


def spread_kernel(halves, out):
    rows = halves[...].reshape(out.shape[1:])
    for index in range(out.shape[0]):
        out[index] = rows


def gather_kernel(blocks, after, out):
    del after
    total = blocks[0].astype(jnp.float32)
    for index in range(1, blocks.shape[0]):
        total = total + blocks[index].astype(jnp.float32)
    width = out.shape[2]
    out[:, 0, :] = total[:, :width].astype(out.dtype)
    out[:, 1, :] = total[:, width:].astype(out.dtype)


def sum_kernel(parts, out):
    total = jnp.sum(parts[...].astype(jnp.float32), axis=0)
    width = parts.shape[2]
    out[:, :width] = total[0:1].astype(out.dtype)
    out[:, width:] = total[1:2].astype(out.dtype)


def hold_kernel(array, out):
    del array, out


def hold(array):
    return pl.pallas_call(
        hold_kernel,
        out_shape=jax.ShapeDtypeStruct(array.shape, array.dtype),
        in_specs=[ANY],
        out_specs=ANY,
        input_output_aliases={0: 0},
        compiler_params=PARAMS,
        cost_estimate=cost(HOLD, 0),
    )(array)


def split_kernel(log_scale, bias, loss_scale, whole, labels, after, *refs, frames):
    del after
    *pieces, rows, tails, sems, tail_sems = refs
    size = pieces[0].shape[0] - TAIL
    stores = []
    for index, piece in enumerate(pieces):
        source = whole.at[pl.ds(index * size, size)]
        target = piece.at[pl.ds(0, size)]
        stores.append(pltpu.make_async_copy(source, target, sems.at[index]))
        stores[-1].start()
    line = lax.broadcasted_iota(jnp.int32, (TAIL, size), 0)
    for index, piece in enumerate(pieces):
        label = labels[:, index * size : (index + 1) * size]
        tail = jnp.where(line == 0, label >> 5, jnp.where(line == 1, label & 31, 0))
        tails[index] = jnp.zeros(tails.shape[1:], tails.dtype)
        tails[index, :, :size] = tail.astype(jnp.float32).astype(tails.dtype)
        target = piece.at[pl.ds(size, TAIL)]
        stores.append(pltpu.make_async_copy(tails.at[index], target, tail_sems.at[index]))
        stores[-1].start()
    factor = jnp.exp(jnp.full((1, rows.shape[1]), log_scale[0]))
    rows[0:1, :] = factor
    rows[1:2, :] = jnp.full(factor.shape, bias[0])
    rows[2:3, :] = factor * loss_scale[0] / frames
    for store in stores:
        store.wait()


def coefficients(block, frames, paired, columns, scalars):
    factor, offset, weight = scalars
    logits = factor * dot(block, frames, (1, 1)) + offset
    own = paired == columns
    value = jax.nn.sigmoid(jnp.where(own, -logits, logits)) * jnp.where(own, -weight, weight)
    return value.astype(jnp.bfloat16)


def scales(rows):
    return rows[0:1, 0:1], rows[1:2, 0:1], rows[2:3, 0:1]


def text_kernel(rows, columns, texts, labels, images, *refs):
    others, (coef, part, *copies, held, load_sem, sems) = refs[:IN_PIECES], refs[IN_PIECES:]
    load = pltpu.make_async_copy(images, held, load_sem)
    load.start()
    stores = []
    for index, copy in enumerate(copies):
        source = texts.at[pl.ds(index * copy.shape[0], copy.shape[0])]
        stores.append(pltpu.make_async_copy(source, copy, sems.at[index]))
        stores[-1].start()
    scalars = scales(rows)
    block = texts[...].reshape(part.shape)
    terms = []
    for piece in others:
        size = piece.shape[0] - TAIL
        frames = piece[:size, :]
        tail = piece[size:, :size].astype(jnp.float32)
        paired = (tail[0:1] * 32 + tail[1:2]).astype(jnp.int32)
        terms.append((coefficients(block, frames, paired, columns[...], scalars), frames))
    load.wait()
    value = coefficients(block, held[...], labels[...], columns[...], scalars)
    coef[...] = value
    terms.append((value, held[...]))
    total = sum(dot(value, frames, (1, 0)) for value, frames in terms)
    part[...] = total.astype(part.dtype)
    for store in stores:
        store.wait()


def image_kernel(rows, columns, labels, coef, texts, images, *refs):
    others, (out, done, result, out_sems) = refs[:TEXT_PIECES], refs[TEXT_PIECES:]
    done[...] = jnp.zeros_like(done)
    scalars = scales(rows)
    block = texts[...].reshape(-1, texts.shape[2])
    other = jnp.concatenate([piece[...] for piece in others], 0).reshape(-1, texts.shape[2])
    size = result.shape[1]
    spans = [slice(index * size, (index + 1) * size) for index in range(result.shape[0])]
    value = coefficients(other, images[...], labels[...], columns[...], scalars)
    stores = []
    for index, span in enumerate(spans):
        total = dot(coef[:, span], block, (0, 0)) + dot(value[:, span], other, (0, 0))
        result[index] = total.astype(result.dtype)
        target = out.at[pl.ds(index * size, size)]
        stores.append(pltpu.make_async_copy(result.at[index], target, out_sems.at[index]))
        stores[-1].start()
    for store in stores:
        store.wait()


def local(images, texts, labels, log_scale, bias, loss_scale):
    far, cores, x, zl = (lax.axis_size(name) for name in ("far", "core", "x", "zl"))
    core = lax.axis_index("core")
    rows = images.shape[0]
    width = texts.shape[1]
    shared = far * x * zl
    frames = rows * shared * cores
    flops = 2 * shared * rows * width

    place = jnp.arange(shared, dtype=jnp.int32)
    first = place // zl % far * (cores * x * zl) + place // (far * zl) * zl + place % zl
    columns = (first + core * x * zl)[:, None]
    columns_other = (first + (1 - core) * x * zl)[:, None]
    half = width // 2
    plane = far * zl

    with jax.named_scope("gather_texts"):
        halves = pl.pallas_call(
            repeat_kernel,
            out_shape=jax.ShapeDtypeStruct((plane, 2, half), texts.dtype),
            in_specs=[VMEM],
            out_specs=VMEM,
            compiler_params=PARAMS,
        )(texts)
        halves = exchange(halves, WIDE)
        blocks = pl.pallas_call(
            spread_kernel,
            out_shape=jax.ShapeDtypeStruct((x, plane, width), texts.dtype),
            in_specs=[VMEM],
            out_specs=VMEM,
            compiler_params=PARAMS,
        )(halves)
        blocks = exchange(blocks, "x")

    with jax.named_scope("swap_images"):
        size = rows // IN_PIECES + TAIL
        *pieces, scale_rows = pl.pallas_call(
            functools.partial(split_kernel, frames=frames),
            out_shape=[pltpu.HBM((size, width), images.dtype)] * IN_PIECES
            + [jax.ShapeDtypeStruct((8, 128), jnp.float32)],
            in_specs=[SMEM] * 3 + [VMEM] * 3,
            out_specs=[HBM] * IN_PIECES + [VMEM],
            scratch_shapes=[
                pltpu.VMEM((IN_PIECES, TAIL, width), images.dtype),
                pltpu.SemaphoreType.DMA((IN_PIECES,)),
                pltpu.SemaphoreType.DMA((IN_PIECES,)),
            ],
            compiler_params=PARAMS,
            cost_estimate=cost(0, 4 * rows * width),
        )(log_scale, bias, loss_scale, *put(pltpu.VMEM, images), labels[None, :], halves)
        others = swap_cores(*pieces)

    with jax.named_scope("coefficients"):
        blocks = hold(blocks)
        coef, part, *copies = pl.pallas_call(
            text_kernel,
            out_shape=(
                jax.ShapeDtypeStruct((shared, rows), jnp.bfloat16),
                jax.ShapeDtypeStruct((shared, width), jnp.bfloat16),
                *[pltpu.HBM((x // TEXT_PIECES, plane, width), blocks.dtype)] * TEXT_PIECES,
            ),
            in_specs=[VMEM] * 4 + [HBM] + [VMEM] * IN_PIECES,
            out_specs=(VMEM, VMEM) + (HBM,) * TEXT_PIECES,
            scratch_shapes=[
                pltpu.VMEM((rows, width), images.dtype),
                pltpu.SemaphoreType.DMA,
                pltpu.SemaphoreType.DMA((TEXT_PIECES,)),
            ],
            compiler_params=PARAMS,
            cost_estimate=cost(4 * flops, 4 * rows * width, 2 * shared * rows),
        )(
            scale_rows,
            columns,
            *put(pltpu.VMEM, blocks),
            labels[None, :],
            *put(pltpu.HBM, images),
            *put(pltpu.VMEM, *others),
        )

    with jax.named_scope("image_grad"):
        copies = swap_cores(*copies)
        image_grad, done = pl.pallas_call(
            image_kernel,
            out_shape=(
                jax.ShapeDtypeStruct((rows, width), jnp.bfloat16),
                jax.ShapeDtypeStruct((8, 128), jnp.float32),
            ),
            in_specs=[VMEM] * (6 + TEXT_PIECES),
            out_specs=(HBM, VMEM),
            scratch_shapes=[
                pltpu.VMEM((OUT_PIECES, rows // OUT_PIECES, width), jnp.bfloat16),
                pltpu.SemaphoreType.DMA((OUT_PIECES,)),
            ],
            compiler_params=PARAMS,
            cost_estimate=cost(0, 0),
        )(scale_rows, columns_other, labels[None, :], coef, blocks, images, *copies)

    with jax.named_scope("text_grad"):
        blocks_grad = exchange(part.reshape(x, plane, width), "x")
        summed = pl.pallas_call(
            gather_kernel,
            out_shape=jax.ShapeDtypeStruct((plane, 2, half), jnp.bfloat16),
            in_specs=[VMEM, VMEM],
            out_specs=VMEM,
            compiler_params=PARAMS,
        )(blocks_grad, done)
        text_grad = pl.pallas_call(
            sum_kernel,
            out_shape=jax.ShapeDtypeStruct((1, width), jnp.bfloat16),
            in_specs=[VMEM],
            out_specs=VMEM,
            compiler_params=PARAMS,
        )(exchange(summed, WIDE))

    return (image_grad, text_grad)


def solution(mesh):
    blk, grp = mesh.devices.shape
    rows = ("far", "core", "x", "zl")
    fine = Mesh(mesh.devices.reshape(blk // 2, 2, 4, grp // 4), rows)
    placed = (P(rows, None), P(rows, None), P(rows), P(), P(), P())
    return jax.shard_map(
        local,
        mesh=fine,
        in_specs=placed,
        out_specs=(P(rows, None), P(rows, None)),
        check_vma=False,
    )
```

```python
import functools

import jax
import jax.numpy as jnp
from jax import lax
from jax.experimental import pallas as pl
from jax.experimental.pallas import tpu as pltpu
from jax.sharding import Mesh
from jax.sharding import PartitionSpec as P

WIDE = ("far", "zl")
IN_PIECES = 2
OUT_PIECES = 2
TEXT_PIECES = 2
TAIL = 16
HOLD = 1 << 34
HBM = pl.BlockSpec(memory_space=pltpu.HBM)
ANY = pl.BlockSpec(memory_space=pl.ANY)
SMEM = pl.BlockSpec(memory_space=pltpu.SMEM)
VMEM = pl.BlockSpec(memory_space=pltpu.VMEM)
PARAMS = pltpu.CompilerParams(vmem_limit_bytes=24 << 20)


def swap_cores(*arrays):
    return [lax.ppermute(array, "core", [(0, 1), (1, 0)]) for array in arrays]


def exchange(array, axes):
    return lax.all_to_all(array, axes, 0, 0, tiled=True)


def dot(left, right, along):
    return lax.dot_general(
        left, right, ((along[:1], along[1:]), ((), ())), preferred_element_type=jnp.float32
    )


def put(space, *arrays):
    return [pltpu.with_memory_space_constraint(array, space) for array in arrays]


def cost(flops, moved, exps=0):
    return pl.CostEstimate(flops=flops, bytes_accessed=moved, transcendentals=exps)


def repeat_kernel(row, out):
    width = out.shape[2]
    values = row[...].astype(jnp.float32)
    halves = jnp.concatenate([values[:, :width], values[:, width:]], 0).astype(out.dtype)
    out[...] = jnp.broadcast_to(halves[None], out.shape)


def spread_kernel(halves, out):
    rows = halves[...].reshape(out.shape[1:])
    for index in range(out.shape[0]):
        out[index] = rows


def gather_kernel(blocks, after, out):
    del after
    total = blocks[0].astype(jnp.float32)
    for index in range(1, blocks.shape[0]):
        total = total + blocks[index].astype(jnp.float32)
    width = out.shape[2]
    out[:, 0, :] = total[:, :width].astype(out.dtype)
    out[:, 1, :] = total[:, width:].astype(out.dtype)


def sum_kernel(parts, out):
    total = jnp.sum(parts[...].astype(jnp.float32), axis=0)
    width = parts.shape[2]
    out[:, :width] = total[0:1].astype(out.dtype)
    out[:, width:] = total[1:2].astype(out.dtype)


def split_kernel(log_scale, bias, loss_scale, whole, labels, after, *refs, frames):
    del after
    *pieces, rows, tails, sems, tail_sems = refs
    size = pieces[0].shape[0] - TAIL
    stores = []
    for index, piece in enumerate(pieces):
        source = whole.at[pl.ds(index * size, size)]
        target = piece.at[pl.ds(0, size)]
        stores.append(pltpu.make_async_copy(source, target, sems.at[index]))
        stores[-1].start()
    line = lax.broadcasted_iota(jnp.int32, (TAIL, size), 0)
    for index, piece in enumerate(pieces):
        label = labels[:, index * size : (index + 1) * size]
        tail = jnp.where(line == 0, label >> 5, jnp.where(line == 1, label & 31, 0))
        tails[index] = jnp.zeros(tails.shape[1:], tails.dtype)
        tails[index, :, :size] = tail.astype(jnp.float32).astype(tails.dtype)
        target = piece.at[pl.ds(size, TAIL)]
        stores.append(pltpu.make_async_copy(tails.at[index], target, tail_sems.at[index]))
        stores[-1].start()
    factor = jnp.exp(jnp.full((1, rows.shape[1]), log_scale[0]))
    rows[0:1, :] = factor
    rows[1:2, :] = jnp.full(factor.shape, bias[0])
    rows[2:3, :] = factor * loss_scale[0] / frames
    for store in stores:
        store.wait()


def coefficients(block, frames, paired, columns, scalars):
    factor, offset, weight = scalars
    logits = factor * dot(block, frames, (1, 1)) + offset
    own = paired == columns
    value = jax.nn.sigmoid(jnp.where(own, -logits, logits)) * jnp.where(own, -weight, weight)
    return value.astype(jnp.bfloat16)


def scales(rows):
    return rows[0:1, 0:1], rows[1:2, 0:1], rows[2:3, 0:1]


def own_kernel(rows, columns, texts, labels, images, coef, *refs):
    *copies, sems = refs
    stores = []
    for index, copy in enumerate(copies):
        source = texts.at[pl.ds(index * copy.shape[0], copy.shape[0])]
        stores.append(pltpu.make_async_copy(source, copy, sems.at[index]))
        stores[-1].start()
    block = texts[...].reshape(-1, texts.shape[2])
    coef[...] = coefficients(block, images[...], labels[...], columns[...], scales(rows))
    for store in stores:
        store.wait()


def text_kernel(rows, columns, texts, coef, images, *refs):
    *others, part = refs
    block = texts[...].reshape(part.shape)
    terms = []
    for piece in others:
        size = piece.shape[0] - TAIL
        frames = piece[:size, :]
        tail = piece[size:, :size].astype(jnp.float32)
        paired = (tail[0:1] * 32 + tail[1:2]).astype(jnp.int32)
        terms.append((coefficients(block, frames, paired, columns[...], scales(rows)), frames))
    terms.append((coef[...], images[...]))
    total = sum(dot(value, frames, (1, 0)) for value, frames in terms)
    part[...] = total.astype(part.dtype)


def image_kernel(rows, columns, labels, coef, texts, images, *refs):
    others, (out, done, result, out_sems) = refs[:TEXT_PIECES], refs[TEXT_PIECES:]
    done[...] = jnp.zeros_like(done)
    scalars = scales(rows)
    block = texts[...].reshape(-1, texts.shape[2])
    other = jnp.concatenate([piece[...] for piece in others], 0).reshape(-1, texts.shape[2])
    size = result.shape[1]
    spans = [slice(index * size, (index + 1) * size) for index in range(result.shape[0])]
    value = coefficients(other, images[...], labels[...], columns[...], scalars)
    stores = []
    for index, span in enumerate(spans):
        total = dot(coef[:, span], block, (0, 0)) + dot(value[:, span], other, (0, 0))
        result[index] = total.astype(result.dtype)
        target = out.at[pl.ds(index * size, size)]
        stores.append(pltpu.make_async_copy(result.at[index], target, out_sems.at[index]))
        stores[-1].start()
    for store in stores:
        store.wait()


def local(images, texts, labels, log_scale, bias, loss_scale):
    far, cores, x, zl = (lax.axis_size(name) for name in ("far", "core", "x", "zl"))
    core = lax.axis_index("core")
    rows = images.shape[0]
    width = texts.shape[1]
    shared = far * x * zl
    frames = rows * shared * cores
    flops = 2 * shared * rows * width

    place = jnp.arange(shared, dtype=jnp.int32)
    first = place // zl % far * (cores * x * zl) + place // (far * zl) * zl + place % zl
    columns = (first + core * x * zl)[:, None]
    columns_other = (first + (1 - core) * x * zl)[:, None]
    half = width // 2
    plane = far * zl

    with jax.named_scope("gather_texts"):
        halves = pl.pallas_call(
            repeat_kernel,
            out_shape=jax.ShapeDtypeStruct((plane, 2, half), texts.dtype),
            in_specs=[VMEM],
            out_specs=VMEM,
            compiler_params=PARAMS,
        )(texts)
        halves = exchange(halves, WIDE)
        blocks = pl.pallas_call(
            spread_kernel,
            out_shape=jax.ShapeDtypeStruct((x, plane, width), texts.dtype),
            in_specs=[VMEM],
            out_specs=VMEM,
            compiler_params=PARAMS,
        )(halves)
        blocks = exchange(blocks, "x")

    with jax.named_scope("swap_images"):
        size = rows // IN_PIECES + TAIL
        *pieces, scale_rows = pl.pallas_call(
            functools.partial(split_kernel, frames=frames),
            out_shape=[pltpu.HBM((size, width), images.dtype)] * IN_PIECES
            + [jax.ShapeDtypeStruct((8, 128), jnp.float32)],
            in_specs=[SMEM] * 3 + [VMEM] * 3,
            out_specs=[HBM] * IN_PIECES + [VMEM],
            scratch_shapes=[
                pltpu.VMEM((IN_PIECES, TAIL, width), images.dtype),
                pltpu.SemaphoreType.DMA((IN_PIECES,)),
                pltpu.SemaphoreType.DMA((IN_PIECES,)),
            ],
            compiler_params=PARAMS,
            cost_estimate=cost(0, 4 * rows * width),
        )(log_scale, bias, loss_scale, *put(pltpu.VMEM, images), labels[None, :], halves)
        others = swap_cores(*pieces)

    with jax.named_scope("coefficients"):
        coef, *copies = pl.pallas_call(
            own_kernel,
            out_shape=(
                jax.ShapeDtypeStruct((shared, rows), jnp.bfloat16),
                *[pltpu.HBM((x // TEXT_PIECES, plane, width), blocks.dtype)] * TEXT_PIECES,
            ),
            in_specs=[VMEM] * 5,
            out_specs=(VMEM,) + (HBM,) * TEXT_PIECES,
            scratch_shapes=[pltpu.SemaphoreType.DMA((TEXT_PIECES,))],
            compiler_params=PARAMS,
            cost_estimate=cost(HOLD, 4 * rows * width, shared * rows),
        )(scale_rows, columns, *put(pltpu.VMEM, blocks), labels[None, :], *put(pltpu.VMEM, images))
        part = pl.pallas_call(
            text_kernel,
            out_shape=jax.ShapeDtypeStruct((shared, width), jnp.bfloat16),
            in_specs=[VMEM] * (5 + IN_PIECES),
            out_specs=VMEM,
            compiler_params=PARAMS,
            cost_estimate=cost(3 * flops, 4 * rows * width, shared * rows),
        )(
            scale_rows,
            columns,
            *put(pltpu.VMEM, blocks, coef, images, *others),
        )

    with jax.named_scope("image_grad"):
        copies = swap_cores(*copies)
        image_grad, done = pl.pallas_call(
            image_kernel,
            out_shape=(
                jax.ShapeDtypeStruct((rows, width), jnp.bfloat16),
                jax.ShapeDtypeStruct((8, 128), jnp.float32),
            ),
            in_specs=[VMEM] * (6 + TEXT_PIECES),
            out_specs=(HBM, VMEM),
            scratch_shapes=[
                pltpu.VMEM((OUT_PIECES, rows // OUT_PIECES, width), jnp.bfloat16),
                pltpu.SemaphoreType.DMA((OUT_PIECES,)),
            ],
            compiler_params=PARAMS,
            cost_estimate=cost(0, 0),
        )(scale_rows, columns_other, labels[None, :], coef, blocks, images, *copies)

    with jax.named_scope("text_grad"):
        blocks_grad = exchange(part.reshape(x, plane, width), "x")
        summed = pl.pallas_call(
            gather_kernel,
            out_shape=jax.ShapeDtypeStruct((plane, 2, half), jnp.bfloat16),
            in_specs=[VMEM, VMEM],
            out_specs=VMEM,
            compiler_params=PARAMS,
        )(blocks_grad, done)
        text_grad = pl.pallas_call(
            sum_kernel,
            out_shape=jax.ShapeDtypeStruct((1, width), jnp.bfloat16),
            in_specs=[VMEM],
            out_specs=VMEM,
            compiler_params=PARAMS,
        )(exchange(summed, WIDE))

    return (image_grad, text_grad)


def solution(mesh):
    blk, grp = mesh.devices.shape
    rows = ("far", "core", "x", "zl")
    fine = Mesh(mesh.devices.reshape(blk // 2, 2, 4, grp // 4), rows)
    placed = (P(rows, None), P(rows, None), P(rows), P(), P(), P())
    return jax.shard_map(
        local,
        mesh=fine,
        in_specs=placed,
        out_specs=(P(rows, None), P(rows, None)),
        check_vma=False,
    )
```

```python
import functools

import jax
import jax.numpy as jnp
from jax import lax
from jax.experimental import pallas as pl
from jax.experimental.pallas import tpu as pltpu
from jax.sharding import Mesh
from jax.sharding import PartitionSpec as P

WIDE = ("far", "zl")
IN_PIECES = 2
OUT_PIECES = 2
TEXT_PIECES = 2
TAIL = 16
HOLD = 1 << 34
HBM = pl.BlockSpec(memory_space=pltpu.HBM)
ANY = pl.BlockSpec(memory_space=pl.ANY)
SMEM = pl.BlockSpec(memory_space=pltpu.SMEM)
VMEM = pl.BlockSpec(memory_space=pltpu.VMEM)
PARAMS = pltpu.CompilerParams(vmem_limit_bytes=24 << 20)


def swap_cores(*arrays):
    return [lax.ppermute(array, "core", [(0, 1), (1, 0)]) for array in arrays]


def exchange(array, axes):
    return lax.all_to_all(array, axes, 0, 0, tiled=True)


def dot(left, right, along):
    return lax.dot_general(
        left, right, ((along[:1], along[1:]), ((), ())), preferred_element_type=jnp.float32
    )


def put(space, *arrays):
    return [pltpu.with_memory_space_constraint(array, space) for array in arrays]


def cost(flops, moved, exps=0):
    return pl.CostEstimate(flops=flops, bytes_accessed=moved, transcendentals=exps)


def repeat_kernel(row, out):
    width = out.shape[2]
    values = row[...].astype(jnp.float32)
    halves = jnp.concatenate([values[:, :width], values[:, width:]], 0).astype(out.dtype)
    out[...] = jnp.broadcast_to(halves[None], out.shape)


def spread_kernel(halves, out):
    rows = halves[...].reshape(out.shape[1:])
    for index in range(out.shape[0]):
        out[index] = rows


def gather_kernel(blocks, after, out):
    del after
    total = blocks[0].astype(jnp.float32)
    for index in range(1, blocks.shape[0]):
        total = total + blocks[index].astype(jnp.float32)
    width = out.shape[2]
    out[:, 0, :] = total[:, :width].astype(out.dtype)
    out[:, 1, :] = total[:, width:].astype(out.dtype)


def sum_kernel(parts, out):
    total = jnp.sum(parts[...].astype(jnp.float32), axis=0)
    width = parts.shape[2]
    out[:, :width] = total[0:1].astype(out.dtype)
    out[:, width:] = total[1:2].astype(out.dtype)


def split_kernel(whole, labels, after, *refs):
    del after
    *pieces, tails, sems, tail_sems = refs
    size = pieces[0].shape[0] - TAIL
    stores = []
    for index, piece in enumerate(pieces):
        source = whole.at[pl.ds(index * size, size)]
        target = piece.at[pl.ds(0, size)]
        stores.append(pltpu.make_async_copy(source, target, sems.at[index]))
        stores[-1].start()
    line = lax.broadcasted_iota(jnp.int32, (TAIL, size), 0)
    for index, piece in enumerate(pieces):
        label = labels[:, index * size : (index + 1) * size]
        tail = jnp.where(line == 0, label >> 5, jnp.where(line == 1, label & 31, 0))
        tails[index] = jnp.zeros(tails.shape[1:], tails.dtype)
        tails[index, :, :size] = tail.astype(jnp.float32).astype(tails.dtype)
        target = piece.at[pl.ds(size, TAIL)]
        stores.append(pltpu.make_async_copy(tails.at[index], target, tail_sems.at[index]))
        stores[-1].start()
    for store in stores:
        store.wait()


def coefficients(block, frames, paired, columns, scalars):
    factor, offset, weight = scalars
    logits = factor * dot(block, frames, (1, 1)) + offset
    own = paired == columns
    value = jax.nn.sigmoid(jnp.where(own, -logits, logits)) * jnp.where(own, -weight, weight)
    return value.astype(jnp.bfloat16)


def scales(rows):
    return rows[0:1, 0:1], rows[1:2, 0:1], rows[2:3, 0:1]


def own_kernel(
    log_scale, bias, loss_scale, columns, texts, labels, images, coef, rows, *refs, frames
):
    *copies, sems = refs
    stores = []
    for index, copy in enumerate(copies):
        source = texts.at[pl.ds(index * copy.shape[0], copy.shape[0])]
        stores.append(pltpu.make_async_copy(source, copy, sems.at[index]))
        stores[-1].start()
    factor = jnp.exp(jnp.full((1, rows.shape[1]), log_scale[0]))
    rows[0:1, :] = factor
    rows[1:2, :] = jnp.full(factor.shape, bias[0])
    rows[2:3, :] = factor * loss_scale[0] / frames
    block = texts[...].reshape(-1, texts.shape[2])
    coef[...] = coefficients(block, images[...], labels[...], columns[...], scales(rows))
    for store in stores:
        store.wait()


def text_kernel(rows, columns, texts, coef, images, *refs):
    *others, part = refs
    block = texts[...].reshape(part.shape)
    terms = []
    for piece in others:
        size = piece.shape[0] - TAIL
        frames = piece[:size, :]
        tail = piece[size:, :size].astype(jnp.float32)
        paired = (tail[0:1] * 32 + tail[1:2]).astype(jnp.int32)
        terms.append((coefficients(block, frames, paired, columns[...], scales(rows)), frames))
    terms.append((coef[...], images[...]))
    total = sum(dot(value, frames, (1, 0)) for value, frames in terms)
    part[...] = total.astype(part.dtype)


def image_kernel(rows, columns, labels, coef, texts, images, *refs):
    others, (out, done, result, out_sems) = refs[:TEXT_PIECES], refs[TEXT_PIECES:]
    done[...] = jnp.zeros_like(done)
    scalars = scales(rows)
    block = texts[...].reshape(-1, texts.shape[2])
    other = jnp.concatenate([piece[...] for piece in others], 0).reshape(-1, texts.shape[2])
    size = result.shape[1]
    spans = [slice(index * size, (index + 1) * size) for index in range(result.shape[0])]
    value = coefficients(other, images[...], labels[...], columns[...], scalars)
    stores = []
    for index, span in enumerate(spans):
        total = dot(coef[:, span], block, (0, 0)) + dot(value[:, span], other, (0, 0))
        result[index] = total.astype(result.dtype)
        target = out.at[pl.ds(index * size, size)]
        stores.append(pltpu.make_async_copy(result.at[index], target, out_sems.at[index]))
        stores[-1].start()
    for store in stores:
        store.wait()


def local(images, texts, labels, log_scale, bias, loss_scale):
    far, cores, x, zl = (lax.axis_size(name) for name in ("far", "core", "x", "zl"))
    core = lax.axis_index("core")
    rows = images.shape[0]
    width = texts.shape[1]
    shared = far * x * zl
    frames = rows * shared * cores
    flops = 2 * shared * rows * width

    place = jnp.arange(shared, dtype=jnp.int32)
    first = place // zl % far * (cores * x * zl) + place // (far * zl) * zl + place % zl
    columns = (first + core * x * zl)[:, None]
    columns_other = (first + (1 - core) * x * zl)[:, None]
    half = width // 2
    plane = far * zl

    with jax.named_scope("gather_texts"):
        halves = pl.pallas_call(
            repeat_kernel,
            out_shape=jax.ShapeDtypeStruct((plane, 2, half), texts.dtype),
            in_specs=[VMEM],
            out_specs=VMEM,
            compiler_params=PARAMS,
        )(texts)
        halves = exchange(halves, WIDE)
        blocks = pl.pallas_call(
            spread_kernel,
            out_shape=jax.ShapeDtypeStruct((x, plane, width), texts.dtype),
            in_specs=[VMEM],
            out_specs=VMEM,
            compiler_params=PARAMS,
        )(halves)
        blocks = exchange(blocks, "x")

    with jax.named_scope("swap_images"):
        size = rows // IN_PIECES + TAIL
        pieces = pl.pallas_call(
            split_kernel,
            out_shape=[pltpu.HBM((size, width), images.dtype)] * IN_PIECES,
            in_specs=[VMEM] * 3,
            out_specs=[HBM] * IN_PIECES,
            scratch_shapes=[
                pltpu.VMEM((IN_PIECES, TAIL, width), images.dtype),
                pltpu.SemaphoreType.DMA((IN_PIECES,)),
                pltpu.SemaphoreType.DMA((IN_PIECES,)),
            ],
            compiler_params=PARAMS,
            cost_estimate=cost(0, 4 * rows * width),
        )(*put(pltpu.VMEM, images), labels[None, :], halves)
        others = swap_cores(*pieces)

    with jax.named_scope("coefficients"):
        coef, scale_rows, *copies = pl.pallas_call(
            functools.partial(own_kernel, frames=frames),
            out_shape=(
                jax.ShapeDtypeStruct((shared, rows), jnp.bfloat16),
                jax.ShapeDtypeStruct((8, 128), jnp.float32),
                *[pltpu.HBM((x // TEXT_PIECES, plane, width), blocks.dtype)] * TEXT_PIECES,
            ),
            in_specs=[SMEM] * 3 + [VMEM] * 4,
            out_specs=(VMEM, VMEM) + (HBM,) * TEXT_PIECES,
            scratch_shapes=[pltpu.SemaphoreType.DMA((TEXT_PIECES,))],
            compiler_params=PARAMS,
            cost_estimate=cost(HOLD, 4 * rows * width, shared * rows),
        )(
            log_scale,
            bias,
            loss_scale,
            columns,
            *put(pltpu.VMEM, blocks),
            labels[None, :],
            *put(pltpu.VMEM, images),
        )
        part = pl.pallas_call(
            text_kernel,
            out_shape=jax.ShapeDtypeStruct((shared, width), jnp.bfloat16),
            in_specs=[VMEM] * (5 + IN_PIECES),
            out_specs=VMEM,
            compiler_params=PARAMS,
            cost_estimate=cost(3 * flops, 4 * rows * width, shared * rows),
        )(
            scale_rows,
            columns,
            *put(pltpu.VMEM, blocks, coef, images, *others),
        )

    with jax.named_scope("image_grad"):
        copies = swap_cores(*copies)
        image_grad, done = pl.pallas_call(
            image_kernel,
            out_shape=(
                jax.ShapeDtypeStruct((rows, width), jnp.bfloat16),
                jax.ShapeDtypeStruct((8, 128), jnp.float32),
            ),
            in_specs=[VMEM] * (6 + TEXT_PIECES),
            out_specs=(HBM, VMEM),
            scratch_shapes=[
                pltpu.VMEM((OUT_PIECES, rows // OUT_PIECES, width), jnp.bfloat16),
                pltpu.SemaphoreType.DMA((OUT_PIECES,)),
            ],
            compiler_params=PARAMS,
            cost_estimate=cost(0, 0),
        )(scale_rows, columns_other, labels[None, :], coef, blocks, images, *copies)

    with jax.named_scope("text_grad"):
        blocks_grad = exchange(part.reshape(x, plane, width), "x")
        summed = pl.pallas_call(
            gather_kernel,
            out_shape=jax.ShapeDtypeStruct((plane, 2, half), jnp.bfloat16),
            in_specs=[VMEM, VMEM],
            out_specs=VMEM,
            compiler_params=PARAMS,
        )(blocks_grad, done)
        text_grad = pl.pallas_call(
            sum_kernel,
            out_shape=jax.ShapeDtypeStruct((1, width), jnp.bfloat16),
            in_specs=[VMEM],
            out_specs=VMEM,
            compiler_params=PARAMS,
        )(exchange(summed, WIDE))

    return (image_grad, text_grad)


def solution(mesh):
    blk, grp = mesh.devices.shape
    rows = ("far", "core", "x", "zl")
    fine = Mesh(mesh.devices.reshape(blk // 2, 2, 4, grp // 4), rows)
    placed = (P(rows, None), P(rows, None), P(rows), P(), P(), P())
    return jax.shard_map(
        local,
        mesh=fine,
        in_specs=placed,
        out_specs=(P(rows, None), P(rows, None)),
        check_vma=False,
    )
```
